32 devices in a mesh: parts: 2 (over y), blk: 8 (over z, x), dp: 2 (over core).
Axes of the slice: x: 2, y: 2, z: 4, core: 2. Of those that a mesh axis runs over, the one named last changes fastest.
Arguments:
- activations: bfloat16 [4, 176, 14336], P(('parts', 'dp'), None, 'blk'), parts along dimension 0, may hold values from -6 to 6
- out_grads: bfloat16 [4, 176, 4096], P(('parts', 'dp'), None, 'blk'), parts along dimension 0, may hold values from -6 to 6
- input_basis: bfloat16 [28672, 14336], P('parts', 'blk'), parts along dimension 0, may hold values from -0.046875 to 0.046875
- output_basis: bfloat16 [8192, 4096], P('parts', 'blk'), parts along dimension 0, may hold values from -0.09375 to 0.09375
Outputs:
- correction: float32 [8192, 14336], P(('parts', 'dp'), 'blk'), parts along dimension 0
The draws below stay inside these ranges and needn't reach their ends.
There are 2 independent parts, one for each index of `parts`. The reference program is written for one: setup_inputs(seed, part) draws one part's arguments, and reference() takes and returns one part's arrays. A program takes and returns all parts, laid end to end along the dimension named above; each array names one. Nothing has to cross between parts.
All inputs are finite; a program needn't handle non-finite values.
Results may differ from the reference program's by a relative error of at most 0.0042.
Values may be sent and summed in bfloat16 or wider, within the bound.
No kernel may reach another device: no remote copies, remote signals or barrier semaphores. Data moves between devices by JAX's collectives and lax.ppermute only.
A program may use at most 256 MiB of HBM per device.

```python
import math
import jax
import jax.numpy as jnp
from jax import lax

FEAT_IN = 14336
FEAT_OUT = 4096
LEN = 176
SEQS = 2


def shard_levels(key, shape, pieces, least, high):
    gain = 1.0
    for dim, parts in pieces:
        steps = jax.random.uniform(jax.random.fold_in(jax.random.fold_in(key, 6), dim), (parts,), jnp.float32, least / len(pieces), high / len(pieces))
        gain = gain * jnp.repeat(jnp.exp(steps), shape[dim] // parts).reshape((-1,) + (1,) * (len(shape) - 1 - dim))
    return gain


def normal_values(rng, extent, spread, reach, cuts=(), held_as=jnp.bfloat16):
    loudness = shard_levels(rng, extent, cuts, -0.22, 0.18) if cuts else 1.0
    values = jax.random.normal(rng, extent, jnp.float32) * spread * loudness
    return jnp.minimum(jnp.maximum(values, -reach), reach).astype(held_as)


def setup_inputs(seed: int = 0, part: int = 0) -> dict:
    splits = jax.random.split(jax.random.key(seed), 5)
    part_splits = jax.random.split(jax.random.fold_in(splits[4], part), 5)
    return {
        "activations": normal_values(part_splits[0], (SEQS, LEN, FEAT_IN), 1.0, 6.0, ((0, 2), (2, 8))),
        "out_grads": normal_values(part_splits[1], (SEQS, LEN, FEAT_OUT), 1.0, 6.0, ((0, 2), (2, 8))),
        "input_basis": normal_values(part_splits[2], (FEAT_IN, FEAT_IN), FEAT_IN ** -0.5, 0.046875, ((1, 8),)),
        "output_basis": normal_values(part_splits[3], (FEAT_OUT, FEAT_OUT), FEAT_OUT ** -0.5, 0.09375, ((1, 8),)),
    }


def reference(activations, out_grads, input_basis, output_basis):
    rotated_in = jnp.dot(activations.reshape(SEQS * LEN, FEAT_IN), input_basis, preferred_element_type=jnp.float32)
    rotated_in = rotated_in.astype(jnp.bfloat16).reshape(SEQS, LEN, FEAT_IN)
    rotated_out = jnp.dot(out_grads.reshape(SEQS * LEN, FEAT_OUT), output_basis, preferred_element_type=jnp.float32)
    rotated_out = rotated_out.astype(jnp.bfloat16).reshape(SEQS, LEN, FEAT_OUT)
    factor = 1.0 / math.sqrt(LEN)

    def add_sequence(running, pair):
        inputs_one, outputs_one = pair
        tile = jnp.dot(outputs_one.T, inputs_one, preferred_element_type=jnp.float32) * factor
        return (running + tile * tile, None)
    start_sum = jnp.zeros((FEAT_OUT, FEAT_IN), jnp.float32)
    summed, unused = lax.scan(add_sequence, start_sum, (rotated_in, rotated_out))
    return summed / SEQS
```

```python
import math

import jax
import jax.numpy as jnp
from jax import lax
from jax.experimental import pallas as pl
from jax.experimental.pallas import tpu as pltpu
from jax.sharding import PartitionSpec as P

SWAP = ((0, 1), (1, 0))
SLAB = 448


def chunk_at(n, q):
    q = lax.rem(q + 2 * n, n)
    return jnp.where(q < n // 2, 2 * q, 2 * n - 1 - 2 * q)


def place_of(n, me):
    return jnp.where(lax.rem(me, 2) == 0, me // 2, n - 1 - me // 2)


def rotate(pieces, distances, offsets, basis, running, last):
    count = len(pieces)
    tokens = pieces[0].shape[0]
    columns = basis.shape[1]
    n = lax.axis_size("blk")
    chunk_rows = basis.shape[0] // n
    slabs = []
    row = 0
    for k in range(count):
        width = pieces[k].shape[1]
        size = SLAB if width % SLAB == 0 else width
        for begin in range(0, width, size):
            slabs.append((k, begin, size, row))
            row += size
    total = row
    has_running = running is not None
    steps = len(slabs)

    def kernel(*refs):
        xs, basis_ref, refs = refs[:count], refs[count], refs[count + 1 :]
        if has_running:
            run_ref, refs = refs[0], refs[1:]
        out_ref, refs = refs[0], refs[1:]
        held, refs = refs[:count], refs[count:]
        slab, acc, sems = refs
        place = place_of(n, lax.axis_index("blk"))
        brought = [pltpu.make_async_copy(xs[k], held[k], sems.at[steps + k]) for k in range(count)]
        copies = []
        for i, (k, begin, size, row) in enumerate(slabs):
            if begin == 0:
                brought[k].start()
            start = pl.multiple_of(chunk_at(n, place + distances[k]) * chunk_rows + offsets[k] + begin, 64)
            copy = pltpu.make_async_copy(basis_ref.at[pl.ds(start, size), :], slab.at[row : row + size, :], sems.at[i])
            copy.start()
            copies.append(copy)
        if has_running:
            run_copy = pltpu.make_async_copy(run_ref, acc, sems.at[steps + count])
            run_copy.start()
        for i, (k, begin, size, row) in enumerate(slabs):
            if begin == 0:
                brought[k].wait()
            copies[i].wait()
            value = jnp.dot(held[k][:, begin : begin + size], slab[row : row + size, :], preferred_element_type=jnp.float32)
            if i == 0 and has_running:
                run_copy.wait()
            if i > 0 or has_running:
                value = acc[...] + value
            if i < steps - 1:
                acc[...] = value
            else:
                out_ref[...] = value.astype(out_ref.dtype)

    whole = pl.BlockSpec(memory_space=pltpu.VMEM)
    anywhere = pl.BlockSpec(memory_space=pl.ANY)
    planned = 2 * total * (columns + tokens) + 8 * tokens * columns
    return pl.pallas_call(
        kernel,
        out_shape=jax.ShapeDtypeStruct((tokens, columns), jnp.bfloat16 if last else jnp.float32),
        in_specs=[anywhere] * (count + 1 + has_running),
        out_specs=whole,
        scratch_shapes=[pltpu.VMEM(p.shape, p.dtype) for p in pieces]
        + [
            pltpu.VMEM((total, columns), basis.dtype),
            pltpu.VMEM((tokens, columns), jnp.float32),
            pltpu.SemaphoreType.DMA((steps + count + 1,)),
        ],
        compiler_params=pltpu.CompilerParams(vmem_limit_bytes=planned + 8 * 1024 * 1024),
        cost_estimate=pl.CostEstimate(
            flops=2 * tokens * total * columns, bytes_accessed=2 * total * columns + 8 * tokens * columns, transcendentals=0
        ),
    )(*pieces, basis, *([running] if has_running else []))


def square_tiles(pieces, distances, offsets, in_mine, in_other, shape, scale, before):
    count = len(pieces)
    tokens, columns = in_mine.shape
    widths = [p[0].shape[1] for p in pieces]
    total = sum(widths)
    has_before = before is not None
    n = lax.axis_size("blk")
    rows_local = shape[0]
    chunk_rows = 2 * rows_local // n
    size = 128

    def kernel(*refs):
        outs, refs = refs[: 2 * count], refs[2 * count :]
        mine_ref, other_ref, refs = refs[0], refs[1], refs[2:]
        if has_before:
            refs = refs[1:]
        out_ref, held, sems = refs
        place = place_of(n, lax.axis_index("blk"))
        starts = [chunk_at(n, place + distances[k]) * chunk_rows + offsets[k] - lax.axis_index("dp") * rows_local for k in range(count)]
        valid = [(start >= 0) & (start < rows_local) for start in starts]

        def copies(k, row):
            start = pl.multiple_of(jnp.where(valid[k], starts[k], 0), size)
            return [
                pltpu.make_async_copy(
                    held.at[pl.ds(row + i * size, size), :], out_ref.at[pl.ds(start + i * size, size), :], sems.at[row // size + i]
                )
                for i in range(widths[k] // size)
            ]

        row = 0
        for k in range(count):

            @pl.when(valid[k])
            def _(k=k, row=row):
                for i, copy in enumerate(copies(k, row)):
                    cols = slice(i * size, (i + 1) * size)
                    first, second = [
                        lax.dot_general(x[:, cols], y[...], (((0,), (0,)), ((), ())), preferred_element_type=jnp.float32)
                        for x, y in ((outs[2 * k], mine_ref), (outs[2 * k + 1], other_ref))
                    ]
                    held[row + i * size : row + (i + 1) * size, :] = (first * first + second * second) * scale
                    copy.start()

            row += widths[k]
        row = 0
        for k in range(count):

            @pl.when(valid[k])
            def _(k=k, row=row):
                for copy in copies(k, row):
                    copy.wait()

            row += widths[k]

    whole = pl.BlockSpec(memory_space=pltpu.VMEM)
    anywhere = pl.BlockSpec(memory_space=pl.ANY)
    return pl.pallas_call(
        kernel,
        out_shape=jax.ShapeDtypeStruct(shape, jnp.float32),
        in_specs=[whole] * (2 * count + 2) + [anywhere] * has_before,
        out_specs=anywhere,
        scratch_shapes=[
            pltpu.VMEM((total, columns), jnp.float32),
            pltpu.SemaphoreType.DMA((total // size,)),
        ],
        input_output_aliases={2 * count + 2: 0} if has_before else {},
        compiler_params=pltpu.CompilerParams(vmem_limit_bytes=4 * total * columns + 16 * 1024 * 1024),
        cost_estimate=pl.CostEstimate(
            flops=2 * tokens * total * columns, bytes_accessed=2 * total * columns, transcendentals=0
        ),
    )(*[x for p in pieces for x in p], in_mine, in_other, *([before] if has_before else []))


def ring_body(activations, out_grads, input_basis, output_basis):
    _, length, in_width = activations.shape
    out_width = out_grads.shape[2]
    acts = activations[0]
    grads = out_grads[0]
    n = lax.axis_size("blk")
    rows_local = n * out_width // 2
    half_in, half_out = in_width // 2, out_width // 2

    path = [2 * q if q < n // 2 else 2 * n - 1 - 2 * q for q in range(n)]
    ahead = [(path[i], path[(i + 1) % n]) for i in range(n)]
    back = [(path[i], path[(i - 1) % n]) for i in range(n)]

    def hop(forward, backward, *after):
        if after:
            forward, backward, _ = lax.optimization_barrier((forward, backward, after))
        return lax.ppermute(forward, "blk", ahead), lax.ppermute(backward, "blk", back)

    def add(total, got, distance):
        return rotate(list(got), (-distance, distance), (0, 0), input_basis, total, False)

    def swap(x):
        return lax.ppermute(x, "dp", SWAP)

    g1 = hop(grads, grads)
    a1 = hop(acts, acts)
    total = rotate([acts], (0,), (0,), input_basis, None, False)
    g2 = hop(*g1, total)
    g3 = hop(*g2)
    a2 = hop(*a1, g2)
    total = add(total, a1, 1)
    g4 = hop(g3[0][:, :half_out], g3[1][:, half_out:], total)
    rotated_out = rotate(
        [grads, *g1, *g2, *g3, *g4], (0, -1, 1, -2, 2, -3, 3, -4, 4), (0,) * 8 + (half_out,), output_basis, None, True
    )
    r1 = hop(rotated_out, rotated_out)
    a3 = hop(*a2, g4)
    total = add(total, a2, 2)
    r2 = hop(*r1, total)
    a4 = hop(a3[0][:, :half_in], a3[1][:, half_in:], r1)
    total = add(total, a3, 3)
    r3 = hop(*r2, total)
    rotated_in = rotate(list(a4), (-4, 4), (0, half_in), input_basis, total, True)
    r4 = hop(r3[0][:, :half_out], r3[1][:, half_out:], rotated_in)
    other_in = swap(rotated_in)
    scale = 1.0 / (length * 2)

    def tiles(pieces, distances, offsets, before):
        pairs = [(p, swap(p)) for p in pieces]
        return square_tiles(pairs, distances, offsets, rotated_in, other_in, (rows_local, in_width), scale, before)

    out = tiles([rotated_out, *r1, *r2], (0, -1, 1, -2, 2), (0,) * 5, None)
    return tiles([*r3, *r4], (-3, 3, -4, 4), (0, 0, 0, half_out), out)


def gather_body(activations, out_grads, input_basis, output_basis):
    seqs, length, _ = activations.shape

    def rotated(x, basis):
        whole = lax.all_gather(x, "blk", axis=2, tiled=True)
        return jnp.einsum("slk,kj->slj", whole, basis, preferred_element_type=jnp.float32).astype(jnp.bfloat16)

    rotated_in = rotated(activations, input_basis)
    rotated_out = lax.all_gather(rotated(out_grads, output_basis), "blk", axis=2, tiled=True)
    tile = jnp.einsum("slp,slj->spj", rotated_out, rotated_in, preferred_element_type=jnp.float32)
    squares = jnp.sum(tile * tile, axis=0)
    summed = lax.psum_scatter(squares, "dp", scatter_dimension=0, tiled=True)
    return summed * (1.0 / (length * seqs * lax.axis_size("dp")))


def solution(mesh):
    placed = (
        P(("parts", "dp"), None, "blk"),
        P(("parts", "dp"), None, "blk"),
        P("parts", "blk"),
        P("parts", "blk"),
    )
    ring = mesh.shape["blk"] == 8 and mesh.shape["dp"] == 2
    body = ring_body if ring else gather_body
    return jax.shard_map(
        body, mesh=mesh, in_specs=placed, out_specs=P(("parts", "dp"), "blk"), check_vma=False
    )
```

```python
import math

import jax
import jax.numpy as jnp
from jax import lax
from jax.experimental import pallas as pl
from jax.experimental.pallas import tpu as pltpu
from jax.sharding import PartitionSpec as P

SWAP = ((0, 1), (1, 0))
SLAB = 448
WEIGHT = 2
LATE = 2


def chunk_at(n, q):
    q = lax.rem(q + 2 * n, n)
    return jnp.where(q < n // 2, 2 * q, 2 * n - 1 - 2 * q)


def place_of(n, me):
    return jnp.where(lax.rem(me, 2) == 0, me // 2, n - 1 - me // 2)


def rotate(pieces, distances, offsets, basis, running, last, weight=WEIGHT):
    count = len(pieces)
    tokens = pieces[0].shape[0]
    columns = basis.shape[1]
    n = lax.axis_size("blk")
    chunk_rows = basis.shape[0] // n
    slabs = []
    row = 0
    for k in range(count):
        width = pieces[k].shape[1]
        size = SLAB if width % SLAB == 0 else width
        for begin in range(0, width, size):
            slabs.append((k, begin, size, row))
            row += size
    total = row
    has_running = running is not None
    steps = len(slabs)

    def kernel(*refs):
        xs, basis_ref, refs = refs[:count], refs[count], refs[count + 1 :]
        if has_running:
            run_ref, refs = refs[0], refs[1:]
        out_ref, refs = refs[0], refs[1:]
        held, refs = refs[:count], refs[count:]
        slab, acc, sems = refs
        place = place_of(n, lax.axis_index("blk"))
        brought = [pltpu.make_async_copy(xs[k], held[k], sems.at[steps + k]) for k in range(count)]
        copies = []
        for i, (k, begin, size, row) in enumerate(slabs):
            if begin == 0:
                brought[k].start()
            start = pl.multiple_of(chunk_at(n, place + distances[k]) * chunk_rows + offsets[k] + begin, 64)
            copy = pltpu.make_async_copy(basis_ref.at[pl.ds(start, size), :], slab.at[row : row + size, :], sems.at[i])
            copy.start()
            copies.append(copy)
        if has_running:
            run_copy = pltpu.make_async_copy(run_ref, acc, sems.at[steps + count])
            run_copy.start()
        for i, (k, begin, size, row) in enumerate(slabs):
            if begin == 0:
                brought[k].wait()
            copies[i].wait()
            value = jnp.dot(held[k][:, begin : begin + size], slab[row : row + size, :], preferred_element_type=jnp.float32)
            if i == 0 and has_running:
                run_copy.wait()
            if i > 0 or has_running:
                value = acc[...] + value
            if i < steps - 1:
                acc[...] = value
            else:
                out_ref[...] = value.astype(out_ref.dtype)

    whole = pl.BlockSpec(memory_space=pltpu.VMEM)
    anywhere = pl.BlockSpec(memory_space=pl.ANY)
    planned = 2 * total * (columns + tokens) + 8 * tokens * columns
    return pl.pallas_call(
        kernel,
        out_shape=jax.ShapeDtypeStruct((tokens, columns), jnp.bfloat16 if last else jnp.float32),
        in_specs=[pl.BlockSpec(memory_space=pltpu.HBM)] * count + [anywhere] * (1 + has_running),
        out_specs=whole,
        scratch_shapes=[pltpu.VMEM(p.shape, p.dtype) for p in pieces]
        + [
            pltpu.VMEM((total, columns), basis.dtype),
            pltpu.VMEM((tokens, columns), jnp.float32),
            pltpu.SemaphoreType.DMA((steps + count + 1,)),
        ],
        compiler_params=pltpu.CompilerParams(vmem_limit_bytes=planned + 8 * 1024 * 1024),
        cost_estimate=pl.CostEstimate(
            flops=2 * weight * tokens * total * columns,
            bytes_accessed=weight * (2 * total * columns + 8 * tokens * columns),
            transcendentals=0,
        ),
    )(*pieces, basis, *([running] if has_running else []))


def square_tiles(pieces, distances, offsets, in_mine, in_other, shape, scale, before):
    count = len(pieces)
    tokens, columns = in_mine.shape
    widths = [p[0].shape[1] for p in pieces]
    total = sum(widths)
    has_before = before is not None
    n = lax.axis_size("blk")
    rows_local = shape[0]
    chunk_rows = 2 * rows_local // n
    size = 128

    def kernel(*refs):
        outs, refs = refs[: 2 * count], refs[2 * count :]
        mine_ref, other_ref, refs = refs[0], refs[1], refs[2:]
        if has_before:
            refs = refs[1:]
        out_ref, held, sems = refs
        place = place_of(n, lax.axis_index("blk"))
        starts = [chunk_at(n, place + distances[k]) * chunk_rows + offsets[k] - lax.axis_index("dp") * rows_local for k in range(count)]
        valid = [(start >= 0) & (start < rows_local) for start in starts]

        def copies(k, row):
            start = pl.multiple_of(jnp.where(valid[k], starts[k], 0), size)
            return [
                pltpu.make_async_copy(
                    held.at[pl.ds(row + i * size, size), :], out_ref.at[pl.ds(start + i * size, size), :], sems.at[row // size + i]
                )
                for i in range(widths[k] // size)
            ]

        row = 0
        for k in range(count):

            @pl.when(valid[k])
            def _(k=k, row=row):
                for i, copy in enumerate(copies(k, row)):
                    cols = slice(i * size, (i + 1) * size)
                    first, second = [
                        lax.dot_general(x[:, cols], y[...], (((0,), (0,)), ((), ())), preferred_element_type=jnp.float32)
                        for x, y in ((outs[2 * k], mine_ref), (outs[2 * k + 1], other_ref))
                    ]
                    held[row + i * size : row + (i + 1) * size, :] = (first * first + second * second) * scale
                    copy.start()

            row += widths[k]
        row = 0
        for k in range(count):

            @pl.when(valid[k])
            def _(k=k, row=row):
                for copy in copies(k, row):
                    copy.wait()

            row += widths[k]

    whole = pl.BlockSpec(memory_space=pltpu.VMEM)
    anywhere = pl.BlockSpec(memory_space=pl.ANY)
    return pl.pallas_call(
        kernel,
        out_shape=jax.ShapeDtypeStruct(shape, jnp.float32),
        in_specs=[whole] * (2 * count + 2) + [anywhere] * has_before,
        out_specs=anywhere,
        scratch_shapes=[
            pltpu.VMEM((total, columns), jnp.float32),
            pltpu.SemaphoreType.DMA((total // size,)),
        ],
        input_output_aliases={2 * count + 2: 0} if has_before else {},
        compiler_params=pltpu.CompilerParams(vmem_limit_bytes=4 * total * columns + 16 * 1024 * 1024),
        cost_estimate=pl.CostEstimate(
            flops=2 * tokens * total * columns, bytes_accessed=2 * total * columns, transcendentals=0
        ),
    )(*[x for p in pieces for x in p], in_mine, in_other, *([before] if has_before else []))


def ring_body(activations, out_grads, input_basis, output_basis):
    _, length, in_width = activations.shape
    out_width = out_grads.shape[2]
    acts = activations[0]
    grads = out_grads[0]
    n = lax.axis_size("blk")
    rows_local = n * out_width // 2
    half_in, half_out = in_width // 2, out_width // 2

    path = [2 * q if q < n // 2 else 2 * n - 1 - 2 * q for q in range(n)]
    ahead = [(path[i], path[(i + 1) % n]) for i in range(n)]
    back = [(path[i], path[(i - 1) % n]) for i in range(n)]

    def after(values, *gates):
        return lax.optimization_barrier((tuple(values), gates))[0]

    def hop(values, *gates):
        forward, backward = after(values, *gates)
        return lax.ppermute(forward, "blk", ahead), lax.ppermute(backward, "blk", back)

    def add(total, pieces, distances, offsets, *gates, last=False, weight=WEIGHT):
        if gates:
            pieces = after(pieces, *gates)
        return rotate(list(pieces), distances, offsets, input_basis, total, last, weight)

    def swap(x):
        return lax.ppermute(x, "dp", SWAP)

    low, high = acts[:, :half_in], acts[:, half_in:]
    first, second = (0, half_in), (half_in, 0)
    g1 = hop((grads, grads))
    a1 = hop((low, high))
    total = add(None, (low, high), (0, 0), first, g1)
    g2 = hop(g1)
    b1 = hop((high, low), a1, total)
    total = add(total, a1, (-1, 1), first, g2)
    g3 = hop(g2)
    a2 = hop(a1, b1, total)
    total = add(total, b1, (-1, 1), second, g3)
    g4 = hop((g3[0][:, :half_out], g3[1][:, half_out:]))
    b2 = hop(b1, a2, total)
    rotated_out = rotate(
        (grads, *g1, *g2, *g3, *g4), (0, -1, 1, -2, 2, -3, 3, -4, 4), (0,) * 8 + (half_out,), output_basis, None, True, 4
    )
    r1 = hop((rotated_out, rotated_out))
    a3 = hop(a2, b2, rotated_out)
    total = add(total, (*a2, *b2), (-2, 2, -2, 2), (*first, *second), r1, weight=1)
    r2 = hop(r1)
    b3 = hop(b2, a3, total)
    r3 = hop(r2)
    a4 = hop(a3, b3)
    total = add(total, (*a3, *b3), (-3, 3, -3, 3), (*first, *second), r3, weight=LATE)
    r4 = hop((r3[0][:, :half_out], r3[1][:, half_out:]))
    mine = (rotated_out, *r1, *r2, *r3, *r4)
    other = [swap(x) for x in (rotated_out, *r1, *r2)]
    other += [swap(x) for x in after((*r3, *r4), total)]
    rotated_in = add(total, a4, (-4, 4), first, other[:5], r4, last=True)
    scale = 1.0 / (length * 2)
    return square_tiles(
        list(zip(mine, other)),
        (0, -1, 1, -2, 2, -3, 3, -4, 4),
        (0,) * 8 + (half_out,),
        rotated_in,
        swap(rotated_in),
        (rows_local, in_width),
        scale,
        None,
    )


def gather_body(activations, out_grads, input_basis, output_basis):
    seqs, length, _ = activations.shape

    def rotated(x, basis):
        whole = lax.all_gather(x, "blk", axis=2, tiled=True)
        return jnp.einsum("slk,kj->slj", whole, basis, preferred_element_type=jnp.float32).astype(jnp.bfloat16)

    rotated_in = rotated(activations, input_basis)
    rotated_out = lax.all_gather(rotated(out_grads, output_basis), "blk", axis=2, tiled=True)
    tile = jnp.einsum("slp,slj->spj", rotated_out, rotated_in, preferred_element_type=jnp.float32)
    squares = jnp.sum(tile * tile, axis=0)
    summed = lax.psum_scatter(squares, "dp", scatter_dimension=0, tiled=True)
    return summed * (1.0 / (length * seqs * lax.axis_size("dp")))


def solution(mesh):
    placed = (
        P(("parts", "dp"), None, "blk"),
        P(("parts", "dp"), None, "blk"),
        P("parts", "blk"),
        P("parts", "blk"),
    )
    ring = mesh.shape["blk"] == 8 and mesh.shape["dp"] == 2
    body = ring_body if ring else gather_body
    return jax.shard_map(
        body, mesh=mesh, in_specs=placed, out_specs=P(("parts", "dp"), "blk"), check_vma=False
    )
```

```python
import math

import jax
import jax.numpy as jnp
from jax import lax
from jax.experimental import pallas as pl
from jax.experimental.pallas import tpu as pltpu
from jax.sharding import PartitionSpec as P

SWAP = ((0, 1), (1, 0))
SLAB = 448
WEIGHT = 2
LATE = 1


def chunk_at(n, q):
    q = lax.rem(q + 2 * n, n)
    return jnp.where(q < n // 2, 2 * q, 2 * n - 1 - 2 * q)


def place_of(n, me):
    return jnp.where(lax.rem(me, 2) == 0, me // 2, n - 1 - me // 2)


def rotate(pieces, distances, offsets, basis, running, last, weight=WEIGHT):
    count = len(pieces)
    tokens = pieces[0].shape[0]
    columns = basis.shape[1]
    n = lax.axis_size("blk")
    chunk_rows = basis.shape[0] // n
    slabs = []
    row = 0
    for k in range(count):
        width = pieces[k].shape[1]
        size = SLAB if width % SLAB == 0 else width
        for begin in range(0, width, size):
            slabs.append((k, begin, size, row))
            row += size
    total = row
    has_running = running is not None
    steps = len(slabs)

    def kernel(*refs):
        xs, basis_ref, refs = refs[:count], refs[count], refs[count + 1 :]
        if has_running:
            run_ref, refs = refs[0], refs[1:]
        out_ref, refs = refs[0], refs[1:]
        held, refs = refs[:count], refs[count:]
        slab, acc, sems = refs
        place = place_of(n, lax.axis_index("blk"))
        brought = [pltpu.make_async_copy(xs[k], held[k], sems.at[steps + k]) for k in range(count)]
        copies = []
        for i, (k, begin, size, row) in enumerate(slabs):
            if begin == 0:
                brought[k].start()
            start = pl.multiple_of(chunk_at(n, place + distances[k]) * chunk_rows + offsets[k] + begin, 64)
            copy = pltpu.make_async_copy(basis_ref.at[pl.ds(start, size), :], slab.at[row : row + size, :], sems.at[i])
            copy.start()
            copies.append(copy)
        if has_running:
            run_copy = pltpu.make_async_copy(run_ref, acc, sems.at[steps + count])
            run_copy.start()
        for i, (k, begin, size, row) in enumerate(slabs):
            if begin == 0:
                brought[k].wait()
            copies[i].wait()
            value = jnp.dot(held[k][:, begin : begin + size], slab[row : row + size, :], preferred_element_type=jnp.float32)
            if i == 0 and has_running:
                run_copy.wait()
            if i > 0 or has_running:
                value = acc[...] + value
            if i < steps - 1:
                acc[...] = value
            else:
                out_ref[...] = value.astype(out_ref.dtype)

    whole = pl.BlockSpec(memory_space=pltpu.VMEM)
    anywhere = pl.BlockSpec(memory_space=pl.ANY)
    planned = 2 * total * (columns + tokens) + 8 * tokens * columns
    return pl.pallas_call(
        kernel,
        out_shape=jax.ShapeDtypeStruct((tokens, columns), jnp.bfloat16 if last else jnp.float32),
        in_specs=[pl.BlockSpec(memory_space=pltpu.HBM)] * count + [anywhere] * (1 + has_running),
        out_specs=whole,
        scratch_shapes=[pltpu.VMEM(p.shape, p.dtype) for p in pieces]
        + [
            pltpu.VMEM((total, columns), basis.dtype),
            pltpu.VMEM((tokens, columns), jnp.float32),
            pltpu.SemaphoreType.DMA((steps + count + 1,)),
        ],
        compiler_params=pltpu.CompilerParams(vmem_limit_bytes=planned + 8 * 1024 * 1024),
        cost_estimate=pl.CostEstimate(
            flops=2 * weight * tokens * total * columns,
            bytes_accessed=weight * (2 * total * columns + 8 * tokens * columns),
            transcendentals=0,
        ),
    )(*pieces, basis, *([running] if has_running else []))


def square_tiles(pieces, distances, offsets, in_mine, in_other, shape, scale, before):
    count = len(pieces)
    tokens, columns = in_mine.shape
    widths = [p[0].shape[1] for p in pieces]
    total = sum(widths)
    has_before = before is not None
    n = lax.axis_size("blk")
    rows_local = shape[0]
    chunk_rows = 2 * rows_local // n
    size = 128

    def kernel(*refs):
        outs, refs = refs[: 2 * count], refs[2 * count :]
        mine_ref, other_ref, refs = refs[0], refs[1], refs[2:]
        if has_before:
            refs = refs[1:]
        out_ref, held, sems = refs
        place = place_of(n, lax.axis_index("blk"))
        starts = [chunk_at(n, place + distances[k]) * chunk_rows + offsets[k] - lax.axis_index("dp") * rows_local for k in range(count)]
        valid = [(start >= 0) & (start < rows_local) for start in starts]

        def copies(k, row):
            start = pl.multiple_of(jnp.where(valid[k], starts[k], 0), size)
            return [
                pltpu.make_async_copy(
                    held.at[pl.ds(row + i * size, size), :], out_ref.at[pl.ds(start + i * size, size), :], sems.at[row // size + i]
                )
                for i in range(widths[k] // size)
            ]

        row = 0
        for k in range(count):

            @pl.when(valid[k])
            def _(k=k, row=row):
                for i, copy in enumerate(copies(k, row)):
                    cols = slice(i * size, (i + 1) * size)
                    first, second = [
                        lax.dot_general(x[:, cols], y[...], (((0,), (0,)), ((), ())), preferred_element_type=jnp.float32)
                        for x, y in ((outs[2 * k], mine_ref), (outs[2 * k + 1], other_ref))
                    ]
                    held[row + i * size : row + (i + 1) * size, :] = (first * first + second * second) * scale
                    copy.start()

            row += widths[k]
        row = 0
        for k in range(count):

            @pl.when(valid[k])
            def _(k=k, row=row):
                for copy in copies(k, row):
                    copy.wait()

            row += widths[k]

    whole = pl.BlockSpec(memory_space=pltpu.VMEM)
    anywhere = pl.BlockSpec(memory_space=pl.ANY)
    return pl.pallas_call(
        kernel,
        out_shape=jax.ShapeDtypeStruct(shape, jnp.float32),
        in_specs=[whole] * (2 * count + 2) + [anywhere] * has_before,
        out_specs=anywhere,
        scratch_shapes=[
            pltpu.VMEM((total, columns), jnp.float32),
            pltpu.SemaphoreType.DMA((total // size,)),
        ],
        input_output_aliases={2 * count + 2: 0} if has_before else {},
        compiler_params=pltpu.CompilerParams(vmem_limit_bytes=4 * total * columns + 16 * 1024 * 1024),
        cost_estimate=pl.CostEstimate(
            flops=2 * tokens * total * columns, bytes_accessed=2 * total * columns, transcendentals=0
        ),
    )(*[x for p in pieces for x in p], in_mine, in_other, *([before] if has_before else []))


def ring_body(activations, out_grads, input_basis, output_basis):
    _, length, in_width = activations.shape
    out_width = out_grads.shape[2]
    acts = activations[0]
    grads = out_grads[0]
    n = lax.axis_size("blk")
    rows_local = n * out_width // 2
    half_in, half_out = in_width // 2, out_width // 2

    path = [2 * q if q < n // 2 else 2 * n - 1 - 2 * q for q in range(n)]
    ahead = [(path[i], path[(i + 1) % n]) for i in range(n)]
    back = [(path[i], path[(i - 1) % n]) for i in range(n)]

    def after(values, *gates):
        return lax.optimization_barrier((tuple(values), gates))[0]

    def hop(values, *gates):
        forward, backward = after(values, *gates)
        return lax.ppermute(forward, "blk", ahead), lax.ppermute(backward, "blk", back)

    def add(total, pieces, distances, offsets, *gates, last=False, weight=WEIGHT):
        if gates:
            pieces = after(pieces, *gates)
        return rotate(list(pieces), distances, offsets, input_basis, total, last, weight)

    def swap(x):
        return lax.ppermute(x, "dp", SWAP)

    low, high = acts[:, :half_in], acts[:, half_in:]
    first, second = (0, half_in), (half_in, 0)
    g1 = hop((grads, grads))
    a1 = hop((low, high))
    total = add(None, (low, high), (0, 0), first, g1)
    g2 = hop(g1)
    b1 = hop((high, low), a1, total)
    total = add(total, a1, (-1, 1), first, g2)
    g3 = hop(g2)
    a2 = hop(a1, b1, total)
    total = add(total, b1, (-1, 1), second, g3)
    g4 = hop((g3[0][:, :half_out], g3[1][:, half_out:]))
    b2 = hop(b1, a2, total)
    rotated_out = rotate(
        (grads, *g1, *g2, *g3, *g4), (0, -1, 1, -2, 2, -3, 3, -4, 4), (0,) * 8 + (half_out,), output_basis, None, True, 4
    )
    r1 = hop((rotated_out, rotated_out))
    a3 = hop(a2, b2, rotated_out)
    total = add(total, (*a2, *b2), (-2, 2, -2, 2), (*first, *second), r1, weight=1)
    r2 = hop(r1)
    b3 = hop(b2, a3, total)
    r3 = hop(r2, total)
    a4 = hop(a3, b3)
    total = add(total, a3, (-3, 3), first, r2, weight=2)
    total = add(total, b3, (-3, 3), second, r3, weight=2)
    r4 = hop((r3[0][:, :half_out], r3[1][:, half_out:]))
    mine = (rotated_out, *r1, *r2, *r3, *r4)
    other = [swap(x) for x in mine]
    rotated_in = add(total, a4, (-4, 4), first, other, last=True)
    scale = 1.0 / (length * 2)
    return square_tiles(
        list(zip(mine, other)),
        (0, -1, 1, -2, 2, -3, 3, -4, 4),
        (0,) * 8 + (half_out,),
        rotated_in,
        swap(rotated_in),
        (rows_local, in_width),
        scale,
        None,
    )


def gather_body(activations, out_grads, input_basis, output_basis):
    seqs, length, _ = activations.shape

    def rotated(x, basis):
        whole = lax.all_gather(x, "blk", axis=2, tiled=True)
        return jnp.einsum("slk,kj->slj", whole, basis, preferred_element_type=jnp.float32).astype(jnp.bfloat16)

    rotated_in = rotated(activations, input_basis)
    rotated_out = lax.all_gather(rotated(out_grads, output_basis), "blk", axis=2, tiled=True)
    tile = jnp.einsum("slp,slj->spj", rotated_out, rotated_in, preferred_element_type=jnp.float32)
    squares = jnp.sum(tile * tile, axis=0)
    summed = lax.psum_scatter(squares, "dp", scatter_dimension=0, tiled=True)
    return summed * (1.0 / (length * seqs * lax.axis_size("dp")))


def solution(mesh):
    placed = (
        P(("parts", "dp"), None, "blk"),
        P(("parts", "dp"), None, "blk"),
        P("parts", "blk"),
        P("parts", "blk"),
    )
    ring = mesh.shape["blk"] == 8 and mesh.shape["dp"] == 2
    body = ring_body if ring else gather_body
    return jax.shard_map(
        body, mesh=mesh, in_specs=placed, out_specs=P(("parts", "dp"), "blk"), check_vma=False
    )
```
